32 devices in a mesh: grp: 2 (over y), ex: 4 (over z), blk: 2 (over x), rep: 2 (over core).
Axes of the slice: x: 2, y: 2, z: 4, core: 2. Of those that a mesh axis runs over, the one named last changes fastest.
Arguments:
- acts: bfloat16 [256, 64, 4096], P(('grp', 'ex'), None, 'blk'), parts along dimension 0, may hold values from -6 to 6
- grads: bfloat16 [256, 64, 4096], P(('grp', 'ex'), None, 'blk'), parts along dimension 0, may hold values from -6 to 6
- lengths: int32 [256], P(('grp', 'ex')), parts along dimension 0, may hold values from 16 to 64
- adapter_down_weight: bfloat16 [4096, 128], P('blk'), may hold values from -0.09375 to 0.09375
- adapter_up_weight: bfloat16 [128, 4096], P(None, 'blk'), may hold values from -0.09375 to 0.09375
- down_random_signs: int32 [4096, 512], P('blk'), may hold values from -1 to 1, as said below
- up_random_signs: int32 [4096, 512], P('blk'), may hold values from -1 to 1, as said below
- mixer: int32 [256, 16], P(None, 'rep'), may hold values from -1 to 1, as said below
- validation_feature_rows: bfloat16 [512, 512, 16], P('ex', 'blk', 'rep'), may hold values from -6 to 6
- validation_task_index: int32 [512], replicated, may hold values from 0 to 7, never falling along the last dimension, each value on 1 to 128 neighbouring positions
Outputs:
- similarity: float32 [256, 512], P(('grp', 'ex')), parts along dimension 0
- task_score: float32 [256, 8], P(('grp', 'ex')), parts along dimension 0
- best: float32 [256], P(('grp', 'ex')), parts along dimension 0
The draws below stay inside these ranges and needn't reach their ends.
There are 2 independent parts, one for each index of `grp`. The reference program is written for one: setup_inputs(seed, part) draws one part's arguments, and reference() takes and returns one part's arrays. A program takes and returns all parts, laid end to end along the dimension named above; an argument that names none is the same for every part. Nothing has to cross between parts.
Inputs may be any that keep to these rules, and one draw needn't show every extreme that they name: `down_random_signs`: every entry is -1 or +1. `up_random_signs`: every entry is -1 or +1. `mixer`: every entry is -1 or +1. `validation_task_index`: ids never fall along the validation examples; every task has at least one and at most 128 examples.
All inputs are finite; a program needn't handle non-finite values.
Results may differ from the reference program's by a relative error of at most 0.013.
Values may be sent and summed in bfloat16 or wider, within the bound.
A program may use at most 128 MiB of HBM per device.

```python
import math
import jax
import jax.numpy as jnp
import numpy as np
from jax import lax

MODEL_WIDTH = 4096
ADAPTER_RANK = 128
KROW = 512
KCOL = 16
NVAL = 512
TASKS = 8
SEQ = 64
EXAMPLES = 128
PROJ = 8192
MOST_TASK = 128


def draw_down_random_signs(key, part):
    key = jax.random.fold_in(key, 11)
    return (2 * jax.random.randint(key, (MODEL_WIDTH, KROW), 0, 2) - 1).astype(jnp.int32)


def draw_up_random_signs(key, part):
    key = jax.random.fold_in(key, 23)
    return (2 * jax.random.randint(key, (MODEL_WIDTH, KROW), 0, 2) - 1).astype(jnp.int32)


def draw_mixer(key, part):
    key = jax.random.fold_in(key, 37)
    return (2 * jax.random.randint(key, (2 * ADAPTER_RANK, KCOL), 0, 2) - 1).astype(jnp.int32)


def set_ends(values, stream_key, smallest, largest):
    dims = values.shape
    index_at = [jax.random.randint(jax.random.fold_in(stream_key, axis), (), 0, dims[axis]) for axis in range(len(dims))]
    values = values.at[tuple(index_at)].set(smallest)
    longest = dims.index(max(dims))
    index_at[longest] = (index_at[longest] + 1) % dims[longest]
    return values.at[tuple(index_at)].set(largest)


def steps_of(own_key, extent, cuts, smallest, top_value):
    level, own = 1.0, jax.random.fold_in(own_key, 6)
    for position, parts in cuts:
        steps = jnp.exp(jax.random.uniform(jax.random.fold_in(own, position), (parts,), jnp.float32, smallest / len(cuts), top_value / len(cuts)))
        level = level * jnp.repeat(steps, extent[position] // parts).reshape([-1 if axis == position else 1 for axis in range(len(extent))])
    return level


def profile(number_of, total, reach, slope):
    weights = [(1 << 20) // math.isqrt(standing ** slope) + 1 for standing in range(2, number_of + 1)]
    surplus, given = total - reach - (number_of - 1), [1] * (number_of - 1)
    while surplus > 0:
        movable = [i for i in range(number_of - 1) if given[i] < reach]
        mass, remaining = sum([weights[i] for i in movable]), surplus
        for i in movable:
            more = min(reach - given[i], max(1, remaining * weights[i] // mass), surplus)
            given[i] = given[i] + more
            surplus = surplus - more
    return np.array([reach] + given)


def ragged(rng, count, total, reach, lean):
    if count == 2:
        one = jax.random.randint(rng, (), max(1, total - reach), min(reach, total - 1) + 1)
        return jnp.stack([one, total - one])
    sizes = jnp.asarray(profile(count, total, reach, lean), jnp.int32)
    pairs = (count - 1) // 2
    giver, sink = sizes[1:1 + 2 * pairs:2], sizes[2:2 + 2 * pairs:2]
    slack = jnp.minimum(giver - 1, reach - sink)
    passed = jax.random.randint(jax.random.fold_in(rng, 1), (pairs,), 0, 1 << 20) % (slack + 1)
    sizes = sizes.at[1:1 + 2 * pairs:2].set(giver - passed).at[2:2 + 2 * pairs:2].set(sink + passed)
    return sizes[jax.random.permutation(jax.random.fold_in(rng, 2), count)]


def gaussian(stream_key, dims, width, bound, pieces=(), kind=jnp.bfloat16):
    result = width * jax.random.normal(stream_key, dims, jnp.float32)
    if pieces:
        result = result * steps_of(stream_key, dims, pieces, -0.22, 0.18)
    return jnp.clip(result, -bound, bound).astype(kind)


def setup_inputs(seed: int = 0, part: int = 0) -> dict:
    seeds = jax.random.split(jax.random.key(seed), 11)
    part_keys = jax.random.split(jax.random.fold_in(seeds[10], part), 11)
    acts = gaussian(part_keys[0], (EXAMPLES, SEQ, MODEL_WIDTH), 1.0, 6.0, ((0, 4), (2, 2)))
    grads = gaussian(part_keys[1], (EXAMPLES, SEQ, MODEL_WIDTH), 1.0, 6.0, ((0, 4), (2, 2)))
    lengths = set_ends(jax.random.randint(part_keys[2], (EXAMPLES,), SEQ // 4, SEQ + 1), jax.random.fold_in(part_keys[2], 1), SEQ // 4, SEQ).astype(jnp.int32)
    adapter_down_weight = gaussian(seeds[3], (MODEL_WIDTH, ADAPTER_RANK), MODEL_WIDTH ** -0.5, 0.09375, ((0, 2),))
    adapter_up_weight = gaussian(seeds[4], (ADAPTER_RANK, MODEL_WIDTH), MODEL_WIDTH ** -0.5, 0.09375, ((1, 2),))
    down_random_signs = draw_down_random_signs(jax.random.fold_in(seeds[10], 71), part)
    up_random_signs = draw_up_random_signs(jax.random.fold_in(seeds[10], 71), part)
    mixer = draw_mixer(jax.random.fold_in(seeds[10], 71), part)
    validation_feature_rows = gaussian(seeds[8], (NVAL, KROW, KCOL), 1.0, 6.0, ((0, 4), (1, 2), (2, 2)))
    validation_task_index = jnp.searchsorted(jnp.cumsum(ragged(seeds[9], TASKS, NVAL, MOST_TASK, 1)), jnp.arange(NVAL), side="right").astype(jnp.int32)
    return dict(acts=acts, grads=grads, lengths=lengths, adapter_down_weight=adapter_down_weight, adapter_up_weight=adapter_up_weight, down_random_signs=down_random_signs, up_random_signs=up_random_signs, mixer=mixer, validation_feature_rows=validation_feature_rows, validation_task_index=validation_task_index)


def single_example_features(single_entry, adapter_down_weight, adapter_up_weight, down_sign_vector, up_sign_vector, mixing_function):
    example_activations, grads_e, length = single_entry
    positions = jnp.arange(SEQ, dtype=jnp.int32)
    token_weight = jnp.where(positions < length, 1.0 / length.astype(jnp.float32), 0.0).astype(jnp.float32)
    weighted_gradient = (grads_e.astype(jnp.float32) * token_weight[:, None]).astype(jnp.bfloat16)
    upward_mixing = jnp.dot(weighted_gradient, adapter_up_weight.T, preferred_element_type=jnp.float32).astype(jnp.bfloat16)
    downward_mixing = jnp.dot(example_activations, adapter_down_weight, preferred_element_type=jnp.float32).astype(jnp.bfloat16)
    grad_a = jnp.dot(example_activations.T, upward_mixing, preferred_element_type=jnp.float32).astype(jnp.bfloat16)
    grad_b = jnp.dot(weighted_gradient.T, downward_mixing, preferred_element_type=jnp.float32).astype(jnp.bfloat16)
    mixed_a = jnp.dot(grad_a, mixing_function[:ADAPTER_RANK], preferred_element_type=jnp.float32).astype(jnp.bfloat16)
    mixed_b = jnp.dot(grad_b, mixing_function[ADAPTER_RANK:], preferred_element_type=jnp.float32).astype(jnp.bfloat16)
    left = jnp.dot(down_sign_vector.T, mixed_a, preferred_element_type=jnp.float32)
    right = jnp.dot(up_sign_vector.T, mixed_b, preferred_element_type=jnp.float32)
    return left + right

def reference(acts, grads, lengths, adapter_down_weight, adapter_up_weight, down_random_signs, up_random_signs, mixer, validation_feature_rows, validation_task_index):
    down_sign_vector = down_random_signs.astype(jnp.bfloat16)
    up_sign_vector = up_random_signs.astype(jnp.bfloat16)
    mixing_function = mixer.astype(jnp.bfloat16)
    feature_rows = lax.map(lambda single_entry: single_example_features(single_entry, adapter_down_weight, adapter_up_weight, down_sign_vector, up_sign_vector, mixing_function), (acts, grads, lengths))
    feature_rows = feature_rows.reshape(feature_rows.shape[0], PROJ)
    feat16 = feature_rows.astype(jnp.bfloat16)
    val_rows = validation_feature_rows.reshape(NVAL, PROJ)
    feat_ms = lax.optimization_barrier(jnp.sum(feature_rows * feature_rows, axis=1)) / PROJ + 1e-06
    val_f = val_rows.astype(jnp.float32)
    val_ms = lax.optimization_barrier(jnp.sum(val_f * val_f, axis=1)) / PROJ + 1e-06
    dots = lax.dot_general(feat16, val_rows, (((1,), (1,)), ((), ())), preferred_element_type=jnp.float32)
    similarity = dots / (jnp.sqrt(jnp.float32(PROJ)) * jnp.sqrt(feat_ms)[:, None] * jnp.sqrt(val_ms)[None, :])
    onehot = (validation_task_index[:, None] == jnp.arange(TASKS, dtype=jnp.int32)[None, :]).astype(jnp.float32)
    count = lax.optimization_barrier(jnp.sum(onehot, axis=0))
    task_score = jnp.dot(similarity, onehot, precision=lax.Precision.HIGHEST) / jnp.sqrt(count)[None, :]
    best = lax.optimization_barrier(jnp.max(task_score, axis=1))
    return (similarity, task_score, best)
```

```python
import functools

import jax
import jax.numpy as jnp
from jax import lax
from jax.experimental import pallas as pl
from jax.experimental.pallas import tpu as pltpu
from jax.sharding import PartitionSpec as P

TASKS = 8
GROUPS = 4
HALVES = 2
SUB = 256
F32 = jnp.float32
BF16 = jnp.bfloat16
MESH = pl.DeviceIdType.MESH
NT = (((1,), (1,)), ((), ()))


def iota(shape, dim):
    return lax.broadcasted_iota(jnp.int32, shape, dim)


def kernel(
    ne, nb, nr, seq, total_proj,
    acts, grads, down_w, up_w, down_s, up_s, val,
    lengths, mixer_t, tasks,
    sim_out, task_out, best_out,
    acts_v, grads_v, down_wv, up_wv, down_sv, up_sv, down_b, up_b, val_v, val_p,
    mix_a, mix_b, pq, part, part16, got, feats, val_sq, feat_sq, dots_s, dots_r,
    load_sem, small_sem, a_send, a_recv, b_send, b_recv, c_send, c_recv,
    v_send, v_recv, f_send, f_recv, e_send, e_recv,
):
    grp, ex = lax.axis_index("grp"), lax.axis_index("ex")
    blk, rep = lax.axis_index("blk"), lax.axis_index("rep")
    nj = nb * nr
    n = ne * nj
    me_j = blk * nr + rep
    me = ex * nj + me_j
    tokens, width = acts_v.shape
    cols = mixer_t.shape[0]
    rank = mixer_t.shape[1] // 2
    own_k = val_v.shape[1]
    nval = val_v.shape[0] // cols
    gtok = tokens // GROUPS
    examples = tokens // seq
    half_ex = examples // HALVES
    half_rows = half_ex * cols
    sub_ex = SUB // seq
    sub_rows = sub_ex * cols

    def at(lin):
        return (grp, lin // nj, lax.rem(lin // nr, nb), lax.rem(lin, nr))

    def local(src, dst, sem):
        c = pltpu.make_async_copy(src, dst, sem)
        c.start()
        return c

    ld_dw = local(down_w, down_wv, small_sem.at[0])
    ld_uw = local(up_w, up_wv, small_sem.at[1])
    ld_g, ld_a = [], []
    for g in range(GROUPS):
        rows = pl.ds(g * gtok, gtok)
        ld_g.append(local(grads.at[rows], grads_v.at[rows], load_sem.at[0, g]))
        ld_a.append(local(acts.at[rows], acts_v.at[rows], load_sem.at[1, g]))
        if g == 1:
            ld_v = local(val, val_v, small_sem.at[2])
            ld_ds = local(down_s, down_sv, small_sem.at[3])
    ld_us = local(up_s, up_sv, small_sem.at[4])

    barrier = pltpu.get_barrier_semaphore()

    def greet(o, carry):
        pl.semaphore_signal(barrier, inc=1, device_id=at(lax.rem(me + o, n)), device_id_type=MESH)
        return carry

    lax.fori_loop(1, n, greet, 0)

    mix = mixer_t[...].astype(F32)
    pad = jnp.zeros((128 - cols, rank), F32)
    mix_u = jnp.concatenate([mix[:, :rank], pad], axis=0).astype(BF16)
    mix_d = jnp.concatenate([mix[:, rank:], pad], axis=0).astype(BF16)
    ld_dw.wait()
    ld_uw.wait()
    wd = lax.dot_general(down_wv[...], mix_d, NT, preferred_element_type=F32).astype(BF16)
    wu = lax.dot_general(
        up_wv[...], mix_u, (((0,), (1,)), ((), ())), preferred_element_type=F32
    ).astype(BF16)

    pl.semaphore_wait(barrier, n - 1)

    def send(src, dst, s, r, lin):
        c = pltpu.make_async_remote_copy(
            src_ref=src, dst_ref=dst, send_sem=s, recv_sem=r, device_id=at(lin), device_id_type=MESH
        )
        c.start()

    def arrived(dst, s, r):
        pltpu.make_async_remote_copy(
            src_ref=dst, dst_ref=dst, send_sem=s, recv_sem=r,
            device_id=at(lax.rem(me + 1, n)), device_id_type=MESH,
        ).wait_recv()

    def left(src, s, r):
        pltpu.make_async_remote_copy(
            src_ref=src, dst_ref=src, send_sem=s, recv_sem=r,
            device_id=at(lax.rem(me + 1, n)), device_id_type=MESH,
        ).wait_send()

    def blk_lin(b):
        return ex * nj + b * nr + rep

    for g in range(GROUPS):
        ld_g[g].wait()
        ld_a[g].wait()
        for i in range(gtok // SUB):
            rows = pl.ds(g * gtok + i * SUB, SUB)
            p = jnp.dot(grads_v[rows, :], wu, preferred_element_type=F32)
            q = jnp.dot(acts_v[rows, :], wd, preferred_element_type=F32)
            lanes = pl.ds(i * SUB, SUB)
            pq[g, blk, 0:cols, lanes] = jnp.transpose(p)[:cols]
            pq[g, blk, cols:2 * cols, lanes] = jnp.transpose(q)[:cols]
        for o in range(1, nb):
            b = lax.rem(blk + o, nb)
            send(pq.at[g, blk], pq.at[g, blk], a_send.at[g, b], a_recv.at[g, blk], blk_lin(b))
        if g == 1:
            ld_v.wait()
            r, c = iota((256, 256), 0), iota((256, 256), 1)
            per = 256 // cols
            perm = jnp.where(lax.rem(r, per) * cols + r // per == c, 1.0, 0.0).astype(BF16)
            ones = jnp.ones((8, own_k), F32)
            for i in range(nval // per):
                piece = jnp.dot(perm, val_v[i * 256:(i + 1) * 256, :], preferred_element_type=F32)
                sq = jnp.zeros((per, own_k), F32)
                for k in range(cols):
                    rows = piece[k * per:(k + 1) * per]
                    val_p[k, i * per:(i + 1) * per, :] = rows.astype(BF16)
                    sq = sq + rows * rows
                val_sq[me_j, :, i * per:(i + 1) * per] = lax.dot_general(
                    ones, sq, NT, preferred_element_type=F32, precision=lax.Precision.HIGHEST
                )
            for o in range(1, nj):
                j = lax.rem(me_j + o, nj)
                send(val_sq.at[me_j], val_sq.at[me_j], v_send.at[j], v_recv.at[me_j], ex * nj + j)
        if g == 2:
            ld_ds.wait()
            down_b[...] = down_sv[...].astype(F32).astype(BF16)
    ld_us.wait()
    up_b[...] = up_sv[...].astype(F32).astype(BF16)

    lane = iota((cols, 128), 1)
    row_ex = iota((sub_rows, SUB), 0) // cols
    lane_ex = iota((sub_rows, SUB), 1) // seq
    diag = row_ex == lane_ex

    def mixed(g):
        for o in range(1, nb):
            b = lax.rem(blk + o, nb)
            arrived(pq.at[g, b], a_send.at[g, b], a_recv.at[g, b])
        both = pq[g, 0]
        for b in range(1, nb):
            both = both + pq[g, b]
        for i in range(gtok // SUB):
            sub = g * (gtok // SUB) + i
            weights = []
            for h in range(SUB // 128):
                e0 = sub * sub_ex + h * (128 // seq)
                size = jnp.where(lane < seq, lengths[e0], lengths[e0 + 1])
                place = jnp.where(lane < seq, lane, lane - seq)
                weights.append(jnp.where(place < size, 1.0 / size.astype(F32), 0.0))
            weight = jnp.concatenate(weights, axis=1)
            rows = pl.ds(sub * SUB, SUB)
            out = pl.ds(sub * sub_rows, sub_rows)
            for first, tok, dst in ((0, acts_v, mix_a), (cols, grads_v, mix_b)):
                x = both[first:first + cols, i * SUB:(i + 1) * SUB] * weight
                x = jnp.where(diag, jnp.concatenate([x] * sub_ex, axis=0), 0.0).astype(BF16)
                dst[out, :] = jnp.dot(x, tok[rows, :], preferred_element_type=F32).astype(BF16)

    def project(h):
        rows = pl.ds(h * half_rows, half_rows)
        res = jnp.dot(mix_a[rows, :], down_b[...], preferred_element_type=F32)
        res = res + jnp.dot(mix_b[rows, :], up_b[...], preferred_element_type=F32)
        for b in range(nb):
            x = res[:, b * own_k:(b + 1) * own_k]
            part[h, b] = x
            part16[h, b] = x.astype(BF16)
        for o in range(1, nb):
            b = lax.rem(blk + o, nb)
            send(part16.at[h, b], got.at[h, blk], b_send.at[h, b], b_recv.at[h, blk], blk_lin(b))

    r, c = iota((half_rows, half_rows), 0), iota((half_rows, half_rows), 1)
    perm_f = jnp.where(lax.rem(r, half_ex) * cols + r // half_ex == c, 1.0, 0.0).astype(BF16)

    def combine(h):
        x = part[h, blk]
        for o in range(1, nb):
            b = lax.rem(blk + o, nb)
            arrived(got.at[h, b], b_send.at[h, b], b_recv.at[h, b])
            x = x + got[h, b].astype(F32)
        feats[ex, h] = jnp.dot(perm_f, x.astype(BF16), preferred_element_type=F32).astype(BF16)
        for o in range(1, ne):
            e = lax.rem(ex + o, ne)
            send(feats.at[ex, h], feats.at[ex, h], c_send.at[h, e], c_recv.at[h, ex], e * nj + me_j)
        sq = jnp.sum((x * x).reshape(half_ex, cols, own_k), axis=1)
        feat_sq[me_j, h * half_ex:(h + 1) * half_ex, :] = jnp.broadcast_to(
            jnp.sum(sq, axis=1, keepdims=True), (half_ex, 128)
        )

    mixed(0)
    mixed(1)
    project(0)
    mixed(2)
    combine(0)
    mixed(3)
    project(1)
    combine(1)
    for o in range(1, nj):
        j = lax.rem(me_j + o, nj)
        send(feat_sq.at[me_j], feat_sq.at[me_j], f_send.at[j], f_recv.at[me_j], ex * nj + j)

    for o in range(1, nj):
        j = lax.rem(me_j + o, nj)
        arrived(val_sq.at[j], v_send.at[j], v_recv.at[j])
    vs = val_sq[0]
    for j in range(1, nj):
        vs = vs + val_sq[j]
    val_scale = (1.0 / jnp.sqrt(vs / total_proj + 1e-06))[0:1]

    for o in range(ne):
        e = lax.rem(ex + ne - o, ne)
        acc = jnp.zeros((examples, nval), F32)
        if o:
            for h in range(HALVES):
                arrived(feats.at[e, h], c_send.at[h, e], c_recv.at[h, e])
        for k in range(cols):
            x = jnp.concatenate(
                [feats[e, h, k * half_ex:(k + 1) * half_ex, :] for h in range(HALVES)], axis=0
            )
            acc = acc + lax.dot_general(x, val_p[k], NT, preferred_element_type=F32)
        dots_s[e] = (acc * val_scale).astype(BF16)
        if o == 0:
            dots_r[ex, me_j] = dots_s[ex]
        for k in range(1 if o == 0 else 0, nj):
            j = lax.rem(me_j + k, nj)
            send(dots_s.at[e], dots_r.at[ex, me_j], e_send.at[e, j], e_recv.at[ex, me_j], e * nj + j)

    for o in range(1, nj):
        j = lax.rem(me_j + o, nj)
        arrived(feat_sq.at[j], f_send.at[j], f_recv.at[j])
    fs = feat_sq[0]
    for j in range(1, nj):
        fs = fs + feat_sq[j]
    feat_scale = 1.0 / (
        jnp.sqrt(F32(total_proj)) * jnp.sqrt(fs[:, 0:1] / total_proj + 1e-06)
    )

    def take(o, carry):
        src = lax.rem(me + o, n)
        e, j = src // nj, lax.rem(src, nj)
        arrived(dots_r.at[e, j], e_send.at[e, j], e_recv.at[e, j])
        return carry

    lax.fori_loop(1, n, take, 0)
    for e in range(ne):
        acc = dots_r[e, 0].astype(F32)
        for j in range(1, nj):
            acc = acc + dots_r[e, j].astype(F32)
        sim_out[:, e * nval:(e + 1) * nval] = acc * feat_scale
    ids = tasks[...]
    onehot = jnp.where(iota((TASKS, ids.shape[1]), 0) == ids, 1.0, 0.0)
    count = jnp.sum(onehot, axis=1, keepdims=True)
    score = lax.dot_general(
        onehot, sim_out[...], NT, preferred_element_type=F32, precision=lax.Precision.HIGHEST
    ) / jnp.sqrt(count)
    task_out[...] = score
    best_out[...] = jnp.max(score, axis=0, keepdims=True)

    for o in range(1, nb):
        b = lax.rem(blk + o, nb)
        for g in range(GROUPS):
            left(pq.at[g, blk], a_send.at[g, b], a_recv.at[g, b])
        for h in range(HALVES):
            left(part16.at[h, b], b_send.at[h, b], b_recv.at[h, b])
    for o in range(1, ne):
        e = lax.rem(ex + o, ne)
        for h in range(HALVES):
            left(feats.at[ex, h], c_send.at[h, e], c_recv.at[h, e])
    for o in range(1, nj):
        j = lax.rem(me_j + o, nj)
        left(val_sq.at[me_j], v_send.at[j], v_recv.at[j])
        left(feat_sq.at[me_j], f_send.at[j], f_recv.at[j])

    def gone(o, carry):
        dst = lax.rem(me + o, n)
        e, j = dst // nj, lax.rem(dst, nj)
        left(dots_s.at[e], e_send.at[e, j], e_recv.at[e, j])
        return carry

    lax.fori_loop(1, n, gone, 0)


def body(
    sizes, acts, grads, lengths, down_w, up_w, down_s, up_s, mixer, val, tasks
):
    ne, nb, nr = sizes
    nj = nb * nr
    examples, seq, width = acts.shape
    tokens = examples * seq
    krow = down_s.shape[1]
    cols = mixer.shape[1]
    nval, own_k, _ = val.shape
    all_val = tasks.shape[0]
    half_rows = examples * cols // HALVES
    rank = down_w.shape[1]
    gtok = tokens // GROUPS
    dma = pltpu.SemaphoreType.DMA
    anyspace = pl.BlockSpec(memory_space=pl.ANY)
    vmem = pl.BlockSpec(memory_space=pltpu.VMEM)
    sim, score, best = pl.pallas_call(
        functools.partial(kernel, ne, nb, nr, seq, float(krow * cols * nr)),
        out_shape=(
            jax.ShapeDtypeStruct((examples, all_val), F32),
            jax.ShapeDtypeStruct((TASKS, examples), F32),
            jax.ShapeDtypeStruct((1, examples), F32),
        ),
        in_specs=[anyspace] * 7 + [pl.BlockSpec(memory_space=pltpu.SMEM), vmem, vmem],
        out_specs=(vmem, vmem, vmem),
        scratch_shapes=[
            pltpu.VMEM((tokens, width), BF16),
            pltpu.VMEM((tokens, width), BF16),
            pltpu.VMEM((width, rank), BF16),
            pltpu.VMEM((rank, width), BF16),
            pltpu.VMEM((width, krow), jnp.int32),
            pltpu.VMEM((width, krow), jnp.int32),
            pltpu.VMEM((width, krow), BF16),
            pltpu.VMEM((width, krow), BF16),
            pltpu.VMEM((nval * cols, own_k), BF16),
            pltpu.VMEM((cols, nval, own_k), BF16),
            pltpu.VMEM((examples * cols, width), BF16),
            pltpu.VMEM((examples * cols, width), BF16),
            pltpu.VMEM((GROUPS, nb, 2 * cols, gtok), F32),
            pltpu.VMEM((HALVES, nb, half_rows, own_k), F32),
            pltpu.VMEM((HALVES, nb, half_rows, own_k), BF16),
            pltpu.VMEM((HALVES, nb, half_rows, own_k), BF16),
            pltpu.VMEM((ne, HALVES, half_rows, own_k), BF16),
            pltpu.VMEM((nj, 8, nval), F32),
            pltpu.VMEM((nj, examples, 128), F32),
            pltpu.VMEM((ne, examples, nval), BF16),
            pltpu.VMEM((ne, nj, examples, nval), BF16),
            dma((2, GROUPS)),
            dma((5,)),
            dma((GROUPS, nb)),
            dma((GROUPS, nb)),
            dma((HALVES, nb)),
            dma((HALVES, nb)),
            dma((HALVES, ne)),
            dma((HALVES, ne)),
            dma((nj,)),
            dma((nj,)),
            dma((nj,)),
            dma((nj,)),
            dma((ne, nj)),
            dma((ne, nj)),
        ],
        compiler_params=pltpu.CompilerParams(
            collective_id=0, has_side_effects=True, vmem_limit_bytes=56 * 1024 * 1024
        ),
    )(
        acts.reshape(tokens, width),
        grads.reshape(tokens, width),
        down_w,
        up_w,
        down_s,
        up_s,
        jnp.transpose(val, (0, 2, 1)).reshape(nval * cols, own_k),
        lengths,
        jnp.transpose(mixer),
        tasks.reshape(1, all_val),
    )
    return sim, jnp.transpose(score), best.reshape(examples)


def solution(mesh):
    placed = (
        P(("grp", "ex"), None, "blk"),
        P(("grp", "ex"), None, "blk"),
        P(("grp", "ex")),
        P("blk", None),
        P(None, "blk"),
        P("blk", None),
        P("blk", None),
        P(None, "rep"),
        P("ex", "blk", "rep"),
        P(),
    )
    sizes = (mesh.shape["ex"], mesh.shape["blk"], mesh.shape["rep"])
    return jax.shard_map(
        functools.partial(body, sizes),
        mesh=mesh,
        in_specs=placed,
        out_specs=(P(("grp", "ex"), None), P(("grp", "ex"), None), P(("grp", "ex"))),
        check_vma=False,
    )
```

```python
import functools

import jax
import jax.numpy as jnp
from jax import lax
from jax.experimental import pallas as pl
from jax.experimental.pallas import tpu as pltpu
from jax.sharding import PartitionSpec as P

TASKS = 8
GROUPS = 4
HALVES = 2
SUB = 256
F32 = jnp.float32
BF16 = jnp.bfloat16
MESH = pl.DeviceIdType.MESH
NT = (((1,), (1,)), ((), ()))


def iota(shape, dim):
    return lax.broadcasted_iota(jnp.int32, shape, dim)


def kernel(
    ne, nb, nr, seq, total_proj,
    acts, grads, down_w, up_w, down_s, up_s, val,
    lengths, mixer_t,
    sim_out,
    acts_v, grads_v, down_wv, up_wv, down_sv, up_sv, down_b, up_b, val_v, val_p,
    mix_a, mix_b, pq, part, part16, got, feats, val_sq, feat_sq, dots_s, dots_r,
    load_sem, small_sem, a_send, a_recv, b_send, b_recv, c_send, c_recv,
    v_send, v_recv, f_send, f_recv, e_send, e_recv,
):
    grp, ex = lax.axis_index("grp"), lax.axis_index("ex")
    blk, rep = lax.axis_index("blk"), lax.axis_index("rep")
    nj = nb * nr
    n = ne * nj
    me_j = blk * nr + rep
    me = ex * nj + me_j
    tokens, width = acts_v.shape
    cols = mixer_t.shape[0]
    rank = mixer_t.shape[1] // 2
    own_k = val_v.shape[1]
    nval = val_v.shape[0] // cols
    gtok = tokens // GROUPS
    examples = tokens // seq
    half_ex = examples // HALVES
    half_rows = half_ex * cols
    sub_ex = SUB // seq
    sub_rows = sub_ex * cols

    def at(lin):
        return (grp, lin // nj, lax.rem(lin // nr, nb), lax.rem(lin, nr))

    def local(src, dst, sem):
        c = pltpu.make_async_copy(src, dst, sem)
        c.start()
        return c

    ld_dw = local(down_w, down_wv, small_sem.at[0])
    ld_uw = local(up_w, up_wv, small_sem.at[1])
    ld_g, ld_a = [], []
    for g in range(GROUPS):
        rows = pl.ds(g * gtok, gtok)
        ld_g.append(local(grads.at[rows], grads_v.at[rows], load_sem.at[0, g]))
        ld_a.append(local(acts.at[rows], acts_v.at[rows], load_sem.at[1, g]))
        if g == GROUPS // 2 - 1:
            ld_ds = local(down_s, down_sv, small_sem.at[3])
            ld_us = local(up_s, up_sv, small_sem.at[4])
    ld_v = local(val, val_v, small_sem.at[2])

    barrier = pltpu.get_barrier_semaphore()

    def greet(o, carry):
        pl.semaphore_signal(barrier, inc=1, device_id=at(lax.rem(me + o, n)), device_id_type=MESH)
        return carry

    lax.fori_loop(1, n, greet, 0)

    mix = mixer_t[...].astype(F32)
    pad = jnp.zeros((128 - cols, rank), F32)
    mix_u = jnp.concatenate([mix[:, :rank], pad], axis=0).astype(BF16)
    mix_d = jnp.concatenate([mix[:, rank:], pad], axis=0).astype(BF16)
    ld_dw.wait()
    ld_uw.wait()
    wd = lax.dot_general(down_wv[...], mix_d, NT, preferred_element_type=F32).astype(BF16)
    wu = lax.dot_general(
        up_wv[...], mix_u, (((0,), (1,)), ((), ())), preferred_element_type=F32
    ).astype(BF16)

    def send(src, dst, s, r, lin):
        c = pltpu.make_async_remote_copy(
            src_ref=src, dst_ref=dst, send_sem=s, recv_sem=r, device_id=at(lin), device_id_type=MESH
        )
        c.start()

    def arrived(dst, s, r):
        pltpu.make_async_remote_copy(
            src_ref=dst, dst_ref=dst, send_sem=s, recv_sem=r,
            device_id=at(lax.rem(me + 1, n)), device_id_type=MESH,
        ).wait_recv()

    def left(src, s, r):
        pltpu.make_async_remote_copy(
            src_ref=src, dst_ref=src, send_sem=s, recv_sem=r,
            device_id=at(lax.rem(me + 1, n)), device_id_type=MESH,
        ).wait_send()

    def blk_lin(b):
        return ex * nj + b * nr + rep

    def rank_space(g):
        ld_g[g].wait()
        ld_a[g].wait()
        for i in range(gtok // SUB):
            rows = pl.ds(g * gtok + i * SUB, SUB)
            p = jnp.dot(grads_v[rows, :], wu, preferred_element_type=F32)
            q = jnp.dot(acts_v[rows, :], wd, preferred_element_type=F32)
            lanes = pl.ds(i * SUB, SUB)
            pq[g, blk, 0:cols, lanes] = jnp.transpose(p)[:cols]
            pq[g, blk, cols:2 * cols, lanes] = jnp.transpose(q)[:cols]
        if g == 0:
            pl.semaphore_wait(barrier, n - 1)
        for o in range(1, nb):
            b = lax.rem(blk + o, nb)
            send(pq.at[g, blk], pq.at[g, blk], a_send.at[g, b], a_recv.at[g, blk], blk_lin(b))

    def validation():
        ld_v.wait()
        r, c = iota((256, 256), 0), iota((256, 256), 1)
        per = 256 // cols
        perm = jnp.where(lax.rem(r, per) * cols + r // per == c, 1.0, 0.0).astype(BF16)
        ones = jnp.ones((8, own_k), F32)
        for i in range(nval // per):
            piece = jnp.dot(perm, val_v[i * 256:(i + 1) * 256, :], preferred_element_type=F32)
            sq = jnp.zeros((per, own_k), F32)
            for k in range(cols):
                rows = piece[k * per:(k + 1) * per]
                val_p[k, i * per:(i + 1) * per, :] = rows.astype(BF16)
                sq = sq + rows * rows
            val_sq[me_j, :, i * per:(i + 1) * per] = lax.dot_general(
                ones, sq, NT, preferred_element_type=F32, precision=lax.Precision.HIGHEST
            )
        for o in range(1, nj):
            j = lax.rem(me_j + o, nj)
            send(val_sq.at[me_j], val_sq.at[me_j], v_send.at[j], v_recv.at[me_j], ex * nj + j)

    lane = iota((cols, 128), 1)
    row_ex = iota((sub_rows, SUB), 0) // cols
    lane_ex = iota((sub_rows, SUB), 1) // seq
    diag = row_ex == lane_ex

    def mixed(g):
        for o in range(1, nb):
            b = lax.rem(blk + o, nb)
            arrived(pq.at[g, b], a_send.at[g, b], a_recv.at[g, b])
        both = pq[g, 0]
        for b in range(1, nb):
            both = both + pq[g, b]
        for i in range(gtok // SUB):
            sub = g * (gtok // SUB) + i
            weights = []
            for h in range(SUB // 128):
                e0 = sub * sub_ex + h * (128 // seq)
                size = jnp.where(lane < seq, lengths[e0], lengths[e0 + 1])
                place = jnp.where(lane < seq, lane, lane - seq)
                weights.append(jnp.where(place < size, 1.0 / size.astype(F32), 0.0))
            weight = jnp.concatenate(weights, axis=1)
            rows = pl.ds(sub * SUB, SUB)
            out = pl.ds(sub * sub_rows, sub_rows)
            for first, tok, dst in ((0, acts_v, mix_a), (cols, grads_v, mix_b)):
                x = both[first:first + cols, i * SUB:(i + 1) * SUB] * weight
                x = jnp.where(diag, jnp.concatenate([x] * sub_ex, axis=0), 0.0).astype(BF16)
                dst[out, :] = jnp.dot(x, tok[rows, :], preferred_element_type=F32).astype(BF16)

    def project(h):
        rows = pl.ds(h * half_rows, half_rows)
        res = jnp.dot(mix_a[rows, :], down_b[...], preferred_element_type=F32)
        res = res + jnp.dot(mix_b[rows, :], up_b[...], preferred_element_type=F32)
        for b in range(nb):
            x = res[:, b * own_k:(b + 1) * own_k]
            part[h, b] = x
            part16[h, b] = x.astype(BF16)
        for o in range(1, nb):
            b = lax.rem(blk + o, nb)
            send(part16.at[h, b], got.at[h, blk], b_send.at[h, b], b_recv.at[h, blk], blk_lin(b))

    r, c = iota((half_rows, half_rows), 0), iota((half_rows, half_rows), 1)
    perm_f = jnp.where(lax.rem(r, half_ex) * cols + r // half_ex == c, 1.0, 0.0).astype(BF16)

    def combine(h):
        x = part[h, blk]
        for o in range(1, nb):
            b = lax.rem(blk + o, nb)
            arrived(got.at[h, b], b_send.at[h, b], b_recv.at[h, b])
            x = x + got[h, b].astype(F32)
        feats[ex, h] = jnp.dot(perm_f, x.astype(BF16), preferred_element_type=F32).astype(BF16)
        for o in range(1, ne):
            e = lax.rem(ex + o, ne)
            send(feats.at[ex, h], feats.at[ex, h], c_send.at[h, e], c_recv.at[h, ex], e * nj + me_j)
        sq = jnp.sum((x * x).reshape(half_ex, cols, own_k), axis=1)
        feat_sq[me_j, h * half_ex:(h + 1) * half_ex, :] = jnp.broadcast_to(
            jnp.sum(sq, axis=1, keepdims=True), (half_ex, 128)
        )

    per_half = GROUPS // HALVES
    for g in range(per_half):
        rank_space(g)
    ld_ds.wait()
    down_b[...] = down_sv[...].astype(F32).astype(BF16)
    ld_us.wait()
    up_b[...] = up_sv[...].astype(F32).astype(BF16)
    for g in range(per_half):
        mixed(g)
    project(0)
    for g in range(per_half, GROUPS):
        rank_space(g)
    combine(0)
    for g in range(per_half, GROUPS):
        mixed(g)
    project(1)
    validation()
    combine(1)
    for o in range(1, nj):
        j = lax.rem(me_j + o, nj)
        send(feat_sq.at[me_j], feat_sq.at[me_j], f_send.at[j], f_recv.at[me_j], ex * nj + j)

    for o in range(1, nj):
        j = lax.rem(me_j + o, nj)
        arrived(val_sq.at[j], v_send.at[j], v_recv.at[j])
    vs = val_sq[0]
    for j in range(1, nj):
        vs = vs + val_sq[j]
    val_scale = (1.0 / jnp.sqrt(vs / total_proj + 1e-06))[0:1]

    for o in range(ne):
        e = lax.rem(ex + ne - o, ne)
        acc = jnp.zeros((examples, nval), F32)
        if o:
            for h in range(HALVES):
                arrived(feats.at[e, h], c_send.at[h, e], c_recv.at[h, e])
        for k in range(cols):
            x = jnp.concatenate(
                [feats[e, h, k * half_ex:(k + 1) * half_ex, :] for h in range(HALVES)], axis=0
            )
            acc = acc + lax.dot_general(x, val_p[k], NT, preferred_element_type=F32)
        dots_s[e] = (acc * val_scale).astype(BF16)
        if o == 0:
            dots_r[ex, me_j] = dots_s[ex]
        for k in range(1 if o == 0 else 0, nj):
            j = lax.rem(me_j + k, nj)
            send(dots_s.at[e], dots_r.at[ex, me_j], e_send.at[e, j], e_recv.at[ex, me_j], e * nj + j)

    for o in range(1, nj):
        j = lax.rem(me_j + o, nj)
        arrived(feat_sq.at[j], f_send.at[j], f_recv.at[j])
    fs = feat_sq[0]
    for j in range(1, nj):
        fs = fs + feat_sq[j]
    feat_scale = 1.0 / (
        jnp.sqrt(F32(total_proj)) * jnp.sqrt(fs[:, 0:1] / total_proj + 1e-06)
    )

    def take(o, carry):
        src = lax.rem(me + o, n)
        e, j = src // nj, lax.rem(src, nj)
        arrived(dots_r.at[e, j], e_send.at[e, j], e_recv.at[e, j])
        return carry

    lax.fori_loop(1, n, take, 0)
    for e in range(ne):
        acc = dots_r[e, 0].astype(F32)
        for j in range(1, nj):
            acc = acc + dots_r[e, j].astype(F32)
        sim_out[:, e * nval:(e + 1) * nval] = acc * feat_scale

    for o in range(1, nb):
        b = lax.rem(blk + o, nb)
        for g in range(GROUPS):
            left(pq.at[g, blk], a_send.at[g, b], a_recv.at[g, b])
        for h in range(HALVES):
            left(part16.at[h, b], b_send.at[h, b], b_recv.at[h, b])
    for o in range(1, ne):
        e = lax.rem(ex + o, ne)
        for h in range(HALVES):
            left(feats.at[ex, h], c_send.at[h, e], c_recv.at[h, e])
    for o in range(1, nj):
        j = lax.rem(me_j + o, nj)
        left(val_sq.at[me_j], v_send.at[j], v_recv.at[j])
        left(feat_sq.at[me_j], f_send.at[j], f_recv.at[j])

    def gone(o, carry):
        dst = lax.rem(me + o, n)
        e, j = dst // nj, lax.rem(dst, nj)
        left(dots_s.at[e], e_send.at[e, j], e_recv.at[e, j])
        return carry

    lax.fori_loop(1, n, gone, 0)


def finish(sim, tasks, sim_out, task_out, best_out):
    ids = tasks[...]
    x = sim[...]
    onehot = jnp.where(iota((TASKS, ids.shape[1]), 0) == ids, 1.0, 0.0)
    count = jnp.sum(onehot, axis=1, keepdims=True)
    score = lax.dot_general(
        onehot, x, NT, preferred_element_type=F32, precision=lax.Precision.HIGHEST
    ) / jnp.sqrt(count)
    sim_out[...] = x
    task_out[...] = score
    best_out[...] = jnp.max(score, axis=0, keepdims=True)


def body(
    sizes, acts, grads, lengths, down_w, up_w, down_s, up_s, mixer, val, tasks
):
    ne, nb, nr = sizes
    nj = nb * nr
    examples, seq, width = acts.shape
    tokens = examples * seq
    krow = down_s.shape[1]
    cols = mixer.shape[1]
    nval, own_k, _ = val.shape
    all_val = tasks.shape[0]
    half_rows = examples * cols // HALVES
    rank = down_w.shape[1]
    gtok = tokens // GROUPS
    dma = pltpu.SemaphoreType.DMA
    anyspace = pl.BlockSpec(memory_space=pl.ANY)
    vmem = pl.BlockSpec(memory_space=pltpu.VMEM)
    raw = pl.pallas_call(
        functools.partial(kernel, ne, nb, nr, seq, float(krow * cols * nr)),
        out_shape=jax.ShapeDtypeStruct((examples, all_val), F32),
        in_specs=[anyspace] * 7 + [pl.BlockSpec(memory_space=pltpu.SMEM), vmem],
        out_specs=vmem,
        scratch_shapes=[
            pltpu.VMEM((tokens, width), BF16),
            pltpu.VMEM((tokens, width), BF16),
            pltpu.VMEM((width, rank), BF16),
            pltpu.VMEM((rank, width), BF16),
            pltpu.VMEM((width, krow), jnp.int32),
            pltpu.VMEM((width, krow), jnp.int32),
            pltpu.VMEM((width, krow), BF16),
            pltpu.VMEM((width, krow), BF16),
            pltpu.VMEM((nval * cols, own_k), BF16),
            pltpu.VMEM((cols, nval, own_k), BF16),
            pltpu.VMEM((examples * cols, width), BF16),
            pltpu.VMEM((examples * cols, width), BF16),
            pltpu.VMEM((GROUPS, nb, 2 * cols, gtok), F32),
            pltpu.VMEM((HALVES, nb, half_rows, own_k), F32),
            pltpu.VMEM((HALVES, nb, half_rows, own_k), BF16),
            pltpu.VMEM((HALVES, nb, half_rows, own_k), BF16),
            pltpu.VMEM((ne, HALVES, half_rows, own_k), BF16),
            pltpu.VMEM((nj, 8, nval), F32),
            pltpu.VMEM((nj, examples, 128), F32),
            pltpu.VMEM((ne, examples, nval), BF16),
            pltpu.VMEM((ne, nj, examples, nval), BF16),
            dma((2, GROUPS)),
            dma((5,)),
            dma((GROUPS, nb)),
            dma((GROUPS, nb)),
            dma((HALVES, nb)),
            dma((HALVES, nb)),
            dma((HALVES, ne)),
            dma((HALVES, ne)),
            dma((nj,)),
            dma((nj,)),
            dma((nj,)),
            dma((nj,)),
            dma((ne, nj)),
            dma((ne, nj)),
        ],
        compiler_params=pltpu.CompilerParams(
            collective_id=0, has_side_effects=True, vmem_limit_bytes=56 * 1024 * 1024
        ),
    )(
        acts.reshape(tokens, width),
        grads.reshape(tokens, width),
        down_w,
        up_w,
        down_s,
        up_s,
        jnp.transpose(val, (0, 2, 1)).reshape(nval * cols, own_k),
        lengths,
        jnp.transpose(mixer),
    )
    sim, score, best = pl.pallas_call(
        finish,
        out_shape=(
            jax.ShapeDtypeStruct((examples, all_val), F32),
            jax.ShapeDtypeStruct((TASKS, examples), F32),
            jax.ShapeDtypeStruct((1, examples), F32),
        ),
        in_specs=[vmem, vmem],
        out_specs=(vmem, vmem, vmem),
    )(raw, tasks.reshape(1, all_val))
    return sim, jnp.transpose(score), best.reshape(examples)


def solution(mesh):
    placed = (
        P(("grp", "ex"), None, "blk"),
        P(("grp", "ex"), None, "blk"),
        P(("grp", "ex")),
        P("blk", None),
        P(None, "blk"),
        P("blk", None),
        P("blk", None),
        P(None, "rep"),
        P("ex", "blk", "rep"),
        P(),
    )
    sizes = (mesh.shape["ex"], mesh.shape["blk"], mesh.shape["rep"])
    return jax.shard_map(
        functools.partial(body, sizes),
        mesh=mesh,
        in_specs=placed,
        out_specs=(P(("grp", "ex"), None), P(("grp", "ex"), None), P(("grp", "ex"))),
        check_vma=False,
    )
```
